32 devices in a mesh: band: 4 (over y, x), dom: 8 (over z, core).
Axes of the slice: x: 2, y: 2, z: 4, core: 2. Of those that a mesh axis runs over, the one named last changes fastest.
Arguments:
- orbitals: bfloat16 [256, 64, 2048], P('dom', None, 'band'), may hold values from -6 to 6
- projector_blocks: bfloat16 [4, 8, 96, 256, 128], P('band', 'dom'), may hold values from -0.1875 to 0.1875
- block_rows: int32 [4, 8, 96], P('band', 'dom'), may hold values from 0 to 15, as said below
- block_cols: int32 [4, 8, 96], P('band', 'dom'), may hold values from 0 to 26
- block_counts: int32 [4, 8], P('band', 'dom'), may hold values from 16 to 96, as said below
- strengths: float32 [9216], P('dom'), may hold values from -1.5 to 1.5
Outputs:
- applied: bfloat16 [256, 64, 2048], P('dom', None, 'band')
The draws below stay inside these ranges and needn't reach their ends.
Inputs may be any that keep to these rules, and one draw needn't show every extreme that they name: `block_rows`: the slots of one device name distinct pairs of row block and column block. `block_counts`: some device has all 96 slots live.
All inputs are finite; a program needn't handle non-finite values.
Results may differ from the reference program's by a relative error of at most 0.0049.
Values may be sent and summed in bfloat16 or wider, within the bound.
No kernel may reach another device: no remote copies, remote signals or barrier semaphores. Data moves between devices by JAX's collectives and lax.ppermute only.
A program may use at most 128 MiB of HBM per device.

```python
import jax
import jax.numpy as jnp
from jax import lax

STATES = 256
ZP = 8
CROSS = 512
RB = 256
CB = 128
CBS = 9
NBMAX = 96
ZN = 64
XR = 2048
PCOL = 1152
N_BAND = 4
N_DOM = 8


def block_pairs(key):
    total = ZP * CROSS // RB * 3 * CBS
    keys = jax.random.split(jax.random.fold_in(key, 7), N_BAND * N_DOM)
    chosen = jax.vmap(lambda single: jax.random.permutation(single, total)[:NBMAX])(keys)
    return chosen.reshape(N_BAND, N_DOM, NBMAX).astype(jnp.int32)


def draw_block_rows(key, part):
    return (block_pairs(key) // (3 * CBS)).astype(jnp.int32)


def draw_block_cols(key, part):
    return (block_pairs(key) % (3 * CBS)).astype(jnp.int32)


def draw_block_counts(key, part):
    lowest = NBMAX // 6
    spread = NBMAX - lowest
    raw = jax.random.randint(jax.random.fold_in(key, 11), (N_BAND, N_DOM), 0, spread + 1)
    loads = lowest + raw * raw * raw // (spread * spread)
    busiest = jax.random.randint(jax.random.fold_in(key, 13), (), 0, N_BAND * N_DOM)
    flat_index = jnp.arange(N_BAND * N_DOM, dtype=jnp.int32).reshape(N_BAND, N_DOM)
    return jnp.where(flat_index == busiest, NBMAX, loads).astype(jnp.int32)


def block_levels(own_key, dims, cuts, least, largest):
    level = 1.0
    for axis_at, shards_of in cuts:
        heights = jax.random.uniform(jax.random.fold_in(jax.random.fold_in(own_key, 6), axis_at), (shards_of,), jnp.float32, least / len(cuts), largest / len(cuts))
        level = level * jnp.repeat(jnp.exp(heights), dims[axis_at] // shards_of).reshape((-1,) + (1,) * (len(dims) - 1 - axis_at))
    return level


def centred(rng, extent, deviation, bound, pieces=(), held_as=jnp.bfloat16):
    factor_of = block_levels(rng, extent, pieces, -0.22, 0.18) if pieces else 1.0
    result = jax.random.normal(rng, extent, jnp.float32) * deviation * factor_of
    return jnp.minimum(jnp.maximum(result, -bound), bound).astype(held_as)


def setup_inputs(seed: int = 0) -> dict:
    splits = jax.random.split(jax.random.key(seed), 7)
    orbitals = centred(splits[0], (STATES, ZN, XR), 1.0, 6.0, ((0, 8), (2, 4)))
    projector_blocks = centred(splits[1], (N_BAND, N_DOM, NBMAX, RB, CB), 1024 ** -0.5, 0.1875, ((0, 4), (1, 8)))
    block_rows = draw_block_rows(jax.random.fold_in(splits[6], 71), 0)
    block_cols = draw_block_cols(jax.random.fold_in(splits[6], 71), 0)
    block_counts = draw_block_counts(jax.random.fold_in(splits[6], 71), 0)
    strengths = jnp.clip(jax.random.uniform(splits[5], (N_DOM * PCOL,), jnp.float32, -1.5, 1.5) * block_levels(splits[5], (N_DOM * PCOL,), ((0, 8),), -0.4, 0.0), -1.5, 1.5)
    return dict(orbitals=orbitals, projector_blocks=projector_blocks, block_rows=block_rows, block_cols=block_cols, block_counts=block_counts, strengths=strengths)


def reference(orbitals, projector_blocks, block_rows, block_cols, block_counts, strengths):
    row_blocks = ZP * CROSS // RB
    devices_all = N_BAND * N_DOM
    by_device = orbitals.reshape(STATES, N_DOM, ZP, N_BAND, CROSS).transpose(3, 1, 0, 2, 4)
    by_device = by_device.reshape(devices_all, STATES, row_blocks, RB)
    weights = projector_blocks.reshape(devices_all, NBMAX, RB, CB)
    slot_rows = block_rows.reshape(devices_all, NBMAX).astype(jnp.int32)
    slot_cols = block_cols.reshape(devices_all, NBMAX).astype(jnp.int32)
    live_counts = block_counts.reshape(devices_all).astype(jnp.int32)
    dom_index = jnp.tile(jnp.arange(N_DOM, dtype=jnp.int32), N_BAND)
    slab_of = (dom_index[:, None] + slot_cols // CBS - 1) % N_DOM
    targets = (slab_of * CBS + slot_cols % CBS).astype(jnp.int32)
    slots = jnp.arange(NBMAX, dtype=jnp.int32)

    def forward(carry, inputs):
        states_dev, weight_dev, rows_dev, count_dev, target_dev = inputs
        picked = jnp.take(states_dev, rows_dev, axis=1)
        term = jnp.einsum('skr,krc->kcs', picked.astype(jnp.float32), weight_dev.astype(jnp.float32))
        weight_live = (slots < count_dev).astype(jnp.float32)
        carry = carry.at[target_dev].add(term * weight_live[:, None, None])
        return carry, None

    start = jnp.zeros((N_DOM * CBS, CB, STATES), jnp.float32)
    coef, _ = lax.scan(forward, start, (by_device, weights, slot_rows, live_counts, targets))
    chi = (strengths.reshape(N_DOM * CBS, CB)[:, :, None] * coef).astype(jnp.bfloat16)

    def backward(carry, inputs):
        weight_dev, rows_dev, count_dev, target_dev = inputs
        chosen = chi[target_dev]
        term = jnp.einsum('krc,kcs->ksr', weight_dev.astype(jnp.float32), chosen.astype(jnp.float32))
        weight_live = (slots < count_dev).astype(jnp.float32)
        term = term * weight_live[:, None, None]
        placed = jnp.zeros((STATES, row_blocks, RB), jnp.float32).at[:, rows_dev, :].add(term.transpose(1, 0, 2))
        return carry, placed.astype(jnp.bfloat16)

    _, outputs = lax.scan(backward, jnp.zeros((), jnp.float32), (weights, slot_rows, live_counts, targets))
    outputs = outputs.reshape(N_BAND, N_DOM, STATES, ZP, CROSS).transpose(2, 1, 3, 0, 4)
    return outputs.reshape(STATES, ZP * N_DOM, CROSS * N_BAND)
```

```python
import jax
import jax.numpy as jnp
from jax import lax
from jax.experimental import pallas as pl
from jax.experimental.pallas import tpu as pltpu
from jax.sharding import PartitionSpec as P

CHUNKS = (16, 16)
DIRECT = True
VMEM_BYTES = 48 * 1024 * 1024
WHOLE = pl.BlockSpec(memory_space=pltpu.VMEM)
SCALARS = pl.BlockSpec(memory_space=pltpu.SMEM)
ANYWHERE = pl.BlockSpec(memory_space=pl.ANY)
CORES = 2


def shifted(value, axis, steps):
    count = lax.axis_size(axis)
    return lax.ppermute(value, axis, [(i, (i + steps) % count) for i in range(count)])


def swapped(value, axis, mask):
    count = lax.axis_size(axis)
    return lax.ppermute(value, axis, [(i, i ^ mask) for i in range(count)])


def each_live(sources, blocks, sems, live, body, width):
    per = sems.shape[1]
    slots = blocks.shape[1]
    step = slots // per

    def copy(side, i):
        span = pl.ds(i * step, step)
        return pltpu.make_async_copy(sources[side].at[span], blocks.at[side, span], sems.at[side, i])

    order = [(side, i) for side in range(len(sources)) for i in range(per)]
    for side, i in order:

        @pl.when(live[side] > i * step)
        def _():
            copy(side, i).start()

    yield
    for side, i in order:
        first = i * step
        here = jnp.clip(live[side] - first, 0, step)
        groups = here // width

        @pl.when(here > 0)
        def _():
            copy(side, i).wait()

        @pl.loop(0, groups)
        def _(g):
            body(side, [first + g * width + t for t in range(width)])

        @pl.loop(groups * width, here)
        def _(k):
            body(side, [first + k])

    yield


def make_project(part_total):
    def kernel(rows, cols, live, origin, *rest):
        parts, rest = rest[:part_total], rest[part_total:]
        sources, after, outs = rest[:CORES], rest[CORES], rest[CORES + 1 : -3]
        blocks, total, sems = rest[-3:]
        width = blocks.shape[2]
        halves = parts[0].shape[2] // width
        count = total.shape[1]

        def body(side, slots):
            terms = []
            for k in slots:
                row = rows[side, k]
                at = pl.ds(pl.multiple_of((row % halves) * width, width), width)
                lhs = [part[row // halves, :, at] for part in parts]
                lhs = lhs[0] if part_total == 1 else jnp.concatenate(lhs, axis=0)
                terms.append(jnp.dot(lhs, blocks[side, k], preferred_element_type=jnp.float32))
            for k, term in zip(slots, terms):
                total[cols[side, k]] += term

        steps = each_live(sources, blocks, sems, live, body, 4)
        next(steps)
        total[...] = jnp.zeros_like(total)
        next(steps)
        share = count // len(outs)
        for mask, out in enumerate(outs):
            start = pl.multiple_of((origin[0] ^ mask) * share, share)
            out[...] = total[:, pl.ds(start, share), :].astype(out.dtype)

    return kernel


def make_apply(part_total):
    def kernel(rows, cols, live, origin, *rest):
        parts, rest = rest[:part_total], rest[part_total:]
        sources, outs = rest[:CORES], rest[CORES + 1 : -3]
        blocks, total, sems = rest[-3:]
        width = blocks.shape[2]
        halves = outs[0].shape[2] // width
        count = total.shape[1]

        def body(side, slots):
            terms = []
            for k in slots:
                lhs = jnp.concatenate([part[cols[side, k]] for part in parts], axis=0)
                terms.append(
                    lax.dot_general(
                        lhs,
                        blocks[side, k],
                        (((1,), (1,)), ((), ())),
                        preferred_element_type=jnp.float32,
                    )
                )
            for k, term in zip(slots, terms):
                total[rows[side, k]] += term

        steps = each_live(sources, blocks, sems, live, body, 4)
        next(steps)
        total[...] = jnp.zeros_like(total)
        next(steps)
        share = count // part_total
        for place in range(part_total):
            start = pl.multiple_of((origin[0] ^ place) * share, share)
            out = outs[place % len(outs)]
            to = pl.ds(0 if len(outs) > 1 else place * share, share)
            for row in range(total.shape[0]):
                at = pl.ds((row % halves) * width, width)
                out[row // halves, to, at] = total[row, pl.ds(start, share), :].astype(out.dtype)

    return kernel


def scratch(weights, total_shape):
    slots = weights.shape[0]
    return [
        pltpu.VMEM((CORES,) + weights.shape, weights.dtype),
        pltpu.VMEM(total_shape, jnp.float32),
        pltpu.SemaphoreType.DMA((CORES, 6 if slots % 6 == 0 else 1)),
    ]


def options(weights, count):
    slots, height, width = weights.shape
    return dict(
        compiler_params=pltpu.CompilerParams(vmem_limit_bytes=VMEM_BYTES),
        cost_estimate=pl.CostEstimate(
            flops=2 * CORES * slots * height * width * count,
            bytes_accessed=CORES * weights.size * 2 + 4 * 1024 * 1024,
            transcendentals=0,
        ),
    )


def project(index, parts, weights, after, col_total, parties):
    count = sum(part.shape[1] for part in parts)
    width = weights[0].shape[2]
    kinds = [jnp.float32] + [jnp.bfloat16] * (parties - 1)
    return pl.pallas_call(
        make_project(len(parts)),
        out_shape=[jax.ShapeDtypeStruct((col_total, count // parties, width), k) for k in kinds],
        in_specs=[SCALARS] * 4 + [WHOLE] * len(parts) + [ANYWHERE] * (CORES + 1),
        out_specs=[WHOLE] * parties,
        scratch_shapes=scratch(weights[0], (col_total, count, width)),
        **options(weights[0], count),
    )(*index, *parts, *weights, after)


def apply(index, parts, weights, after, shapes):
    planes, _, points = shapes[0]
    count = sum(shape[1] for shape in shapes)
    height = weights[0].shape[1]
    return pl.pallas_call(
        make_apply(len(parts)),
        out_shape=[jax.ShapeDtypeStruct(shape, jnp.bfloat16) for shape in shapes],
        in_specs=[SCALARS] * 4 + [WHOLE] * len(parts) + [ANYWHERE] * (CORES + 1),
        out_specs=[WHOLE] * len(shapes),
        scratch_shapes=scratch(weights[0], (planes * points // height, count, height)),
        **options(weights[0], count),
    )(*index, *parts, *weights, after)


def per_device(orbitals, projector_blocks, block_rows, block_cols, block_counts, strengths):
    slabs = lax.axis_size("dom")
    parties = lax.axis_size("band")
    chips = slabs // CORES
    local, all_planes, points = orbitals.shape
    planes = all_planes // chips
    weights = projector_blocks[0, 0]
    slots, height, width = weights.shape
    col_blocks = strengths.shape[0] // width
    row_blocks = planes * points // height // CORES
    band = lax.axis_index("band").astype(jnp.int32)
    place = lax.axis_index("dom").astype(jnp.int32)
    core, chip = place % CORES, place // CORES
    direct = DIRECT and chips == parties and all(size % 16 == 0 for size in CHUNKS)
    sizes = CHUNKS if direct and sum(CHUNKS) == local else (local,)

    def across(value, steps):
        return shifted(value, "dom", CORES * steps)

    def bring(piece):
        if direct:
            parts = []
            for mask in range(chips):
                start = (chip ^ mask) * planes
                part = lax.dynamic_slice_in_dim(piece, start, planes, axis=1).transpose(1, 0, 2)
                parts.append(swapped(part, "dom", CORES * mask) if mask else part)
            return parts
        size = piece.shape[0]
        piece = piece.reshape(size, chips, planes, points).transpose(1, 2, 0, 3)
        groups = [[CORES * i + c for i in range(chips)] for c in range(CORES)]
        states = lax.all_to_all(piece, "dom", 0, 0, axis_index_groups=groups, tiled=True)
        return [states.transpose(1, 0, 2, 3).reshape(planes, chips * size, points)]

    def returned(parts, size):
        if direct:
            parts = [parts[0]] + [swapped(part, "dom", CORES * m) for m, part in enumerate(parts) if m]
            whole = jnp.zeros((size, all_planes, points), jnp.bfloat16)
            for mask, part in enumerate(parts):
                start = (chip ^ mask) * planes
                whole = lax.dynamic_update_slice_in_dim(whole, part.transpose(1, 0, 2), start, axis=1)
            return whole
        result = parts[0].reshape(planes, chips, size, points).transpose(1, 0, 2, 3)
        groups = [[CORES * i + c for i in range(chips)] for c in range(CORES)]
        result = lax.all_to_all(result, "dom", 0, 0, axis_index_groups=groups, tiled=True)
        return result.reshape(all_planes, size, points).transpose(1, 0, 2)

    numbers = jnp.concatenate(
        [
            block_rows.reshape(-1).astype(jnp.float32),
            block_cols.reshape(-1).astype(jnp.float32),
            block_counts.reshape(-1).astype(jnp.float32),
            strengths,
        ]
    )
    pair = jnp.stack([numbers, swapped(numbers, "dom", 1)])
    sides = jnp.stack([core, 1 - core])[:, None]
    index = (
        pair[:, :slots].astype(jnp.int32) + sides * row_blocks,
        pair[:, slots : 2 * slots].astype(jnp.int32) + sides * col_blocks,
        pair[:, 2 * slots].astype(jnp.int32),
        (band ^ chip if direct else band).reshape(1),
    )
    scaling = pair[:, 2 * slots + 1 :]
    scaling = jnp.where(core == 0, scaling, scaling[::-1]).reshape(CORES, col_blocks, 1, width)
    both = (weights, swapped(weights, "dom", 1))

    def summed(shares):
        partial = shares[0]
        for mask, share in enumerate(shares[1:], 1):
            partial = partial + swapped(share, "band", mask).astype(jnp.float32)
        return partial.reshape(CORES + 2, col_blocks, *partial.shape[1:])

    def scaled(partial):
        below = across(partial[CORES + 1], 1)
        above = across(partial[0], -1)
        own = [partial[1] + below, partial[CORES] + above]
        return (scaling * jnp.stack(own)).astype(jnp.bfloat16)

    def gathered(chi):
        near = jnp.concatenate([across(chi[CORES - 1 :], 1), chi, across(chi[:1], -1)], axis=0)
        near = near.reshape(-1, *near.shape[2:])
        return [near] + [swapped(near, "band", mask) for mask in range(1, parties)]

    chis, shapes, token = [], [], strengths
    first = 0
    for size in sizes:
        parts = bring(orbitals[first : first + size])
        first += size
        shapes.append([part.shape for part in parts])
        partial = summed(project(index, parts, both, token, (CORES + 2) * col_blocks, parties))
        token = partial
        chis.append(scaled(partial))
    finished = []
    for size, shape, chi in zip(sizes, shapes, chis):
        result = apply(index, gathered(chi), both, chis[-1], shape)
        finished.append(returned(result, size))
    return finished[0] if len(finished) == 1 else jnp.concatenate(finished, axis=0)


def solution(mesh):
    return jax.shard_map(
        per_device,
        mesh=mesh,
        in_specs=(
            P("dom", None, "band"),
            P("band", "dom", None, None, None),
            P("band", "dom", None),
            P("band", "dom", None),
            P("band", "dom"),
            P("dom"),
        ),
        out_specs=P("dom", None, "band"),
        check_vma=False,
    )
```

```python
import jax
import jax.numpy as jnp
from jax import lax
from jax.experimental import pallas as pl
from jax.experimental.pallas import tpu as pltpu
from jax.sharding import PartitionSpec as P

CHUNKS = (16, 16)
DIRECT = True
NEAR = 1
AFTER = 0
LAST = 1
ORDER = (3, 2, 1, 0)
HOLD = (2,)
PINNED = True
VMEM_BYTES = 24 * 1024 * 1024
SMALL_BYTES = 8 * 1024 * 1024
WIDTH = 8
WHOLE = pl.BlockSpec(memory_space=pltpu.VMEM)
SCALARS = pl.BlockSpec(memory_space=pltpu.SMEM)
ANYWHERE = pl.BlockSpec(memory_space=pl.ANY)
APART = pl.BlockSpec(memory_space=pltpu.HBM) if PINNED else ANYWHERE
CORES = 2


def shifted(value, axis, steps):
    count = lax.axis_size(axis)
    return lax.ppermute(value, axis, [(i, (i + steps) % count) for i in range(count)])


def swapped(value, axis, mask):
    count = lax.axis_size(axis)
    return lax.ppermute(value, axis, [(i, i ^ mask) for i in range(count)])


def each_pair(sources, blocks, sems, live, pairs, meanwhile, body):
    per = sems.shape[1]
    step = blocks.shape[1] // per

    def each_copy(side, act):
        for i in range(per):
            span = pl.ds(i * step, step)

            @pl.when(live[side] > i * step)
            def _():
                copy = pltpu.make_async_copy(sources[side].at[span], blocks.at[side, span], sems.at[side, i])
                act(copy)

    for side in range(len(sources)):
        each_copy(side, lambda copy: copy.start())
    meanwhile()
    for side in range(len(sources)):
        each_copy(side, lambda copy: copy.wait())

        @pl.loop(0, (pairs[side] + WIDTH - 1) // WIDTH)
        def _(g):
            body(side, [g * WIDTH + t for t in range(WIDTH)])


def paired(rows, cols, live, row_blocks, spare):
    slots = rows.shape[1]
    slot = jnp.arange(slots, dtype=jnp.int32)
    place_total = -(-(slots + row_blocks) // 2 // WIDTH) * WIDTH
    alive = slot[None] < live[:, None]
    same = (rows[:, :, None] == rows[:, None, :]) & alive[:, None, :]
    rank = jnp.sum(same & (slot[None, None, :] < slot[None, :, None]), axis=2, dtype=jnp.int32)
    opens = alive & (rank % 2 == 0)
    lower = opens[:, None, :] & (rows[:, None, :] < rows[:, :, None])
    pair = jnp.sum(lower, axis=2, dtype=jnp.int32) + rank // 2
    here = pair[:, None, :] == jnp.arange(place_total, dtype=jnp.int32)[None, :, None]
    first = here & opens[:, None, :]
    second = here & (alive & (rank % 2 == 1))[:, None, :]

    def of(mask, values, default):
        found = jnp.sum(jnp.where(mask, values[:, None, :] - default, 0), axis=2, dtype=jnp.int32)
        return found + default

    slots_of = jnp.broadcast_to(slot[None], rows.shape)
    return (
        of(first, rows, 0),
        of(first, slots_of, 0),
        of(second, slots_of, 0),
        of(first, cols, spare),
        of(second, cols, spare),
        jnp.sum(opens, axis=1, dtype=jnp.int32),
        live,
    )


def make_project(starts, count, out_total):
    def kernel(rows, firsts, seconds, first_cols, second_cols, pairs, live, origin, *rest):
        parts, rest = rest[: len(starts)], rest[len(starts) :]
        sources, outs = rest[:CORES], rest[-3 - out_total : -3]
        blocks, total, sems = rest[-3:]
        width, depth = blocks.shape[2:]
        halves = parts[0].shape[2] // width
        size = count // len(starts)

        def meanwhile():
            total[...] = jnp.zeros_like(total)

        def body(side, places):
            terms = []
            for p in places:
                row = rows[side, p]
                at = pl.ds(pl.multiple_of((row % halves) * width, width), width)
                lhs = [part[row // halves, pl.ds(s, size), at] for part, s in zip(parts, starts)]
                lhs = lhs[0] if len(lhs) == 1 else jnp.concatenate(lhs, axis=0)
                rhs = [blocks[side, firsts[side, p]], blocks[side, seconds[side, p]]]
                rhs = jnp.concatenate(rhs, axis=1)
                terms.append(jnp.dot(lhs, rhs, preferred_element_type=jnp.float32))
            for p, term in zip(places, terms):
                total[first_cols[side, p]] += term[:, :depth]
                total[second_cols[side, p]] += term[:, depth:]

        each_pair(sources, blocks, sems, live, pairs, meanwhile, body)
        share = count // len(outs)
        for mask, out in enumerate(outs):
            start = pl.multiple_of((origin[0] ^ mask) * share, share)
            out[...] = total[: out.shape[0], pl.ds(start, share), :].astype(out.dtype)

    return kernel


def make_apply(part_total, earlier_total, out_total):
    def kernel(rows, firsts, seconds, first_cols, second_cols, pairs, live, origin, *rest):
        parts, rest = rest[:part_total], rest[part_total:]
        sources, rest = rest[:CORES], rest[CORES:]
        earlier, outs = rest[:earlier_total], rest[-4 - out_total : -4]
        blocks, chi, total, sems = rest[-4:]
        width = blocks.shape[2]
        halves = outs[0].shape[2] // width
        count = total.shape[1]
        share = count // part_total

        def meanwhile():
            total[...] = jnp.zeros_like(total)
            spare = parts[0].shape[0]
            chi[spare] = jnp.zeros_like(chi[spare])
            for mask, part in enumerate(parts):
                chi[:spare, mask * share : (mask + 1) * share, :] = part[...]
            for value, out in zip(earlier, outs):
                out[:, : value.shape[1], :] = value[...]

        def body(side, places):
            terms = []
            for p in places:
                lhs = jnp.concatenate([chi[first_cols[side, p]], chi[second_cols[side, p]]], axis=1)
                rhs = [blocks[side, firsts[side, p]], blocks[side, seconds[side, p]]]
                rhs = jnp.concatenate(rhs, axis=1)
                dims = (((1,), (1,)), ((), ()))
                terms.append(lax.dot_general(lhs, rhs, dims, preferred_element_type=jnp.float32))
            for p, term in zip(places, terms):
                total[rows[side, p]] += term

        each_pair(sources, blocks, sems, live, pairs, meanwhile, body)
        for place in range(part_total):
            start = pl.multiple_of((origin[0] ^ place) * share, share)
            out = outs[place % len(outs)]
            to = pl.ds(out.shape[1] - share if len(outs) > 1 else place * share, share)
            for row in range(total.shape[0]):
                at = pl.ds((row % halves) * width, width)
                out[row // halves, to, at] = total[row, pl.ds(start, share), :].astype(out.dtype)

    return kernel


def options(weights, count):
    slots, height, width = weights.shape
    return dict(
        compiler_params=pltpu.CompilerParams(vmem_limit_bytes=VMEM_BYTES),
        cost_estimate=pl.CostEstimate(
            flops=2 * CORES * slots * height * width * count,
            bytes_accessed=CORES * weights.size * 2 + 4 * 1024 * 1024,
            transcendentals=0,
        ),
    )


def held(weights):
    slots = weights[0].shape[0]
    return (
        pltpu.VMEM((CORES,) + weights[0].shape, weights[0].dtype),
        pltpu.SemaphoreType.DMA((CORES, 6 if slots % 6 == 0 else 1)),
    )


def project(index, parts, starts, count, weights, after, col_total, parties):
    width = weights[0].shape[2]
    blocks, sems = held(weights)
    kinds = [jnp.float32] + [jnp.bfloat16] * (parties - 1)
    return pl.pallas_call(
        make_project(starts, count, parties),
        out_shape=[jax.ShapeDtypeStruct((col_total, count // parties, width), k) for k in kinds],
        in_specs=[SCALARS] * len(index) + [WHOLE] * len(parts) + [APART] * CORES + [ANYWHERE] * len(after),
        out_specs=[WHOLE] * parties,
        scratch_shapes=[blocks, pltpu.VMEM((col_total + 1, count, width), jnp.float32), sems],
        **options(weights[0], count),
    )(*index, *parts, *weights, *after)


def add_kernel(own, *rest):
    scaling, low, high = rest[-3:]
    value = own[...]
    for share in rest[:-3]:
        value = value + share[...].astype(jnp.float32)
    half = value.shape[0] // 2
    cols = scaling.shape[0] // CORES
    low[:half] = value[:half]
    high[:half] = value[half:]
    low[half, :cols] = scaling[:cols]
    high[half, :cols] = scaling[cols:]


def added(shares, scaling):
    total, rows, width = shares[0].shape
    shape = jax.ShapeDtypeStruct((total // 2 + 1, rows, width), jnp.float32)
    return pl.pallas_call(
        add_kernel,
        out_shape=[shape, shape],
        in_specs=[WHOLE] * (len(shares) + 1),
        out_specs=[WHOLE] * 2,
        compiler_params=pltpu.CompilerParams(vmem_limit_bytes=SMALL_BYTES),
    )(*shares, scaling)


def scale_kernel(low, high, below, above, out):
    half = low.shape[0] - 1
    cols = half // 2
    for at, own, other, couplings in (
        (0, low, below, (below, low)),
        (half, high, above, (high, above)),
    ):
        for side, source in enumerate(couplings):
            for c in range(cols):
                k = side * cols + c
                scale = source[half, c : c + 1, :]
                out[at + k] = (scale * (own[k] + other[k])).astype(jnp.bfloat16)


def scaled(low, high, below, above):
    blocks, rows, width = low.shape
    return pl.pallas_call(
        scale_kernel,
        out_shape=jax.ShapeDtypeStruct((2 * (blocks - 1), rows, width), jnp.bfloat16),
        in_specs=[WHOLE] * 4,
        out_specs=WHOLE,
        compiler_params=pltpu.CompilerParams(vmem_limit_bytes=SMALL_BYTES),
    )(low, high, below, above)


def apply(index, parts, weights, earlier, after, shapes):
    planes, _, points = shapes[0]
    col_total, rows, width = parts[0].shape
    count = rows * len(parts)
    height = weights[0].shape[1]
    blocks, sems = held(weights)
    return pl.pallas_call(
        make_apply(len(parts), len(earlier), len(shapes)),
        out_shape=[jax.ShapeDtypeStruct(shape, jnp.bfloat16) for shape in shapes],
        in_specs=[SCALARS] * len(index)
        + [WHOLE] * len(parts)
        + [APART] * CORES
        + [WHOLE] * len(earlier)
        + [ANYWHERE] * len(after),
        out_specs=[WHOLE] * len(shapes),
        scratch_shapes=[
            blocks,
            pltpu.VMEM((col_total + 1, count, width), jnp.bfloat16),
            pltpu.VMEM((planes * points // height, count, height), jnp.float32),
            sems,
        ],
        **options(weights[0], count),
    )(*index, *parts, *weights, *earlier, *after)


def per_device(orbitals, projector_blocks, block_rows, block_cols, block_counts, strengths):
    slabs = lax.axis_size("dom")
    parties = lax.axis_size("band")
    chips = slabs // CORES
    local, all_planes, points = orbitals.shape
    planes = all_planes // chips
    weights = projector_blocks[0, 0]
    slots, height, width = weights.shape
    col_blocks = strengths.shape[0] // width
    row_blocks = planes * points // height // CORES
    band = lax.axis_index("band").astype(jnp.int32)
    place = lax.axis_index("dom").astype(jnp.int32)
    core, chip = place % CORES, place // CORES
    sizes = CHUNKS if sum(CHUNKS) == local else (local,)
    direct = DIRECT and chips == parties and all(size % 16 == 0 for size in sizes)
    sizes = sizes if direct else (local,)
    firsts = [sum(sizes[:i]) for i in range(len(sizes))]

    def across(value, steps):
        return shifted(value, "dom", CORES * steps)

    groups = [[CORES * i + c for i in range(chips)] for c in range(CORES)]

    def taken(source, first, size, mask):
        piece = lax.dynamic_slice(source, (first, (chip ^ mask) * planes, 0), (size, planes, points))
        return piece.transpose(1, 0, 2)

    def brought():
        if not direct:
            piece = orbitals.reshape(local, chips, planes, points).transpose(1, 2, 0, 3)
            states = lax.all_to_all(piece, "dom", 0, 0, axis_index_groups=groups, tiled=True)
            return [([states.transpose(1, 0, 2, 3).reshape(planes, chips * local, points)], [0])]
        source, near, far = orbitals, {}, [{} for _ in sizes]
        for chunk, (first, size) in enumerate(zip(firsts, sizes)):
            for mask in ORDER:
                if mask <= NEAR and chunk:
                    continue
                span = (0, local) if mask <= NEAR else (first, size)
                piece = taken(source, *span, mask)
                (near if mask <= NEAR else far[chunk])[mask] = piece
        near = {mask: swapped(piece, "dom", CORES * mask) if mask else piece for mask, piece in near.items()}
        for chunk, pieces in enumerate(far):
            masks = [mask for mask in ORDER if mask in pieces]
            if chunk and HOLD:
                earlier = far[chunk - 1]
                tied = [pieces[mask] for mask in masks] + [earlier[mask] for mask in HOLD]
                tied = lax.optimization_barrier(tuple(tied))
                pieces.update(zip(masks, tied))
                earlier.update(zip(HOLD, tied[len(masks) :]))
            for mask in masks:
                pieces[mask] = swapped(pieces[mask], "dom", CORES * mask)
        chunks = []
        for first, pieces in zip(firsts, far):
            held_in = [near.get(mask, pieces.get(mask)) for mask in range(chips)]
            chunks.append((held_in, [first if mask <= NEAR else 0 for mask in range(chips)]))
        return chunks

    def returned(results):
        if not direct:
            result = results[0][0].reshape(planes, chips, local, points).transpose(1, 0, 2, 3)
            result = lax.all_to_all(result, "dom", 0, 0, axis_index_groups=groups, tiled=True)
            return result.reshape(all_planes, local, points).transpose(1, 0, 2)
        pieces = []
        for first, size, result in zip(firsts, sizes, results):
            for mask in range(NEAR + 1, chips):
                pieces.append((first, mask, swapped(result[mask], "dom", CORES * mask)))
        for mask in range(NEAR + 1):
            part = results[-1][mask]
            pieces.append((0, mask, swapped(part, "dom", CORES * mask) if mask else part))
        whole = jnp.zeros(orbitals.shape, orbitals.dtype)
        for first, mask, part in pieces:
            start = (first, (chip ^ mask) * planes, 0)
            whole = lax.dynamic_update_slice(whole, part.transpose(1, 0, 2), start)
        return whole

    numbers = jnp.concatenate(
        [
            block_rows.reshape(-1).astype(jnp.float32),
            block_cols.reshape(-1).astype(jnp.float32),
            block_counts.reshape(-1).astype(jnp.float32),
            strengths,
        ]
    )
    pair = jnp.stack([numbers, swapped(numbers, "dom", 1)])
    sides = jnp.stack([core, 1 - core])[:, None]
    index = paired(
        pair[:, :slots].astype(jnp.int32) + sides * row_blocks,
        pair[:, slots : 2 * slots].astype(jnp.int32) + sides * col_blocks,
        pair[:, 2 * slots].astype(jnp.int32),
        row_blocks,
        (CORES + 2) * col_blocks,
    )
    index = index + ((band ^ chip if direct else band).reshape(1),)
    scaling = pair[:, 2 * slots + 1 :]
    ends = [jnp.where(core == c, scaling[0], scaling[1]) for c in range(CORES)]
    scaling = jnp.concatenate(ends).reshape(CORES * col_blocks, width)
    both = (weights, swapped(weights, "dom", 1))

    col_total = (CORES + 2) * col_blocks
    chis, token = [], []
    for size, (parts, starts) in zip(sizes, brought()):
        count = size * chips
        own, *sends = project(index, parts, starts, count, both, token, col_total, parties)
        shares = [swapped(send, "band", mask) for mask, send in enumerate(sends, 1)]
        low, high = added([own] + shares, scaling)
        below, above = lax.optimization_barrier((across(high, 1), across(low, -1)))
        chi = scaled(low, high, below, above)
        parts = [chi] + [swapped(chi, "band", mask) for mask in range(1, parties)]
        chis.append(parts)
        token = [(low, chi, parts[-1])[AFTER]]
        lasts = [[], [low], [chi]][LAST]
    results, earlier = [], []
    for first, size, parts in zip(firsts, sizes, chis):
        if direct:
            shapes = [(planes, size + (first if mask <= NEAR else 0), points) for mask in range(chips)]
        else:
            shapes = [(planes, chips * size, points)]
        results.append(apply(index, parts, both, earlier, lasts, shapes))
        earlier = results[-1][: NEAR + 1]
    return returned(results)


def solution(mesh):
    return jax.shard_map(
        per_device,
        mesh=mesh,
        in_specs=(
            P("dom", None, "band"),
            P("band", "dom", None, None, None),
            P("band", "dom", None),
            P("band", "dom", None),
            P("band", "dom"),
            P("dom"),
        ),
        out_specs=P("dom", None, "band"),
        check_vma=False,
    )
```

```python
import jax
import jax.numpy as jnp
from jax import lax
from jax.experimental import pallas as pl
from jax.experimental.pallas import tpu as pltpu
from jax.sharding import PartitionSpec as P

CHUNKS = (16, 16)
DIRECT = True
NEAR = 1
AFTER = 0
LAST = 1
RESIDENT = 1
ORDER = (3, 2, 1, 0)
HOLD = (2,)
PINNED = True
VMEM_BYTES = 24 * 1024 * 1024
SMALL_BYTES = 8 * 1024 * 1024
WIDTH = 8
WHOLE = pl.BlockSpec(memory_space=pltpu.VMEM)
SCALARS = pl.BlockSpec(memory_space=pltpu.SMEM)
ANYWHERE = pl.BlockSpec(memory_space=pl.ANY)
APART = pl.BlockSpec(memory_space=pltpu.HBM) if PINNED else ANYWHERE
CORES = 2


def shifted(value, axis, steps):
    count = lax.axis_size(axis)
    return lax.ppermute(value, axis, [(i, (i + steps) % count) for i in range(count)])


def swapped(value, axis, mask):
    count = lax.axis_size(axis)
    return lax.ppermute(value, axis, [(i, i ^ mask) for i in range(count)])


def each_pair(sources, blocks, sems, live, pairs, meanwhile, body, resident=0):
    per = sems.shape[1]
    step = blocks.shape[1] // per

    def each_copy(side, act):
        for i in range(per):
            span = pl.ds(i * step, step)

            @pl.when(live[side] > i * step)
            def _():
                copy = pltpu.make_async_copy(sources[side].at[span], blocks.at[side, span], sems.at[side, i])
                act(copy)

    for side in range(resident, len(sources)):
        each_copy(side, lambda copy: copy.start())
    meanwhile()
    for side in range(len(sources)):
        if side >= resident:
            each_copy(side, lambda copy: copy.wait())

        @pl.loop(0, (pairs[side] + WIDTH - 1) // WIDTH)
        def _(g):
            body(side, [g * WIDTH + t for t in range(WIDTH)])


def paired(rows, cols, live, row_blocks, spare):
    slots = rows.shape[1]
    slot = jnp.arange(slots, dtype=jnp.int32)
    place_total = -(-(slots + row_blocks) // 2 // WIDTH) * WIDTH
    alive = slot[None] < live[:, None]
    same = (rows[:, :, None] == rows[:, None, :]) & alive[:, None, :]
    rank = jnp.sum(same & (slot[None, None, :] < slot[None, :, None]), axis=2, dtype=jnp.int32)
    opens = alive & (rank % 2 == 0)
    lower = opens[:, None, :] & (rows[:, None, :] < rows[:, :, None])
    pair = jnp.sum(lower, axis=2, dtype=jnp.int32) + rank // 2
    here = pair[:, None, :] == jnp.arange(place_total, dtype=jnp.int32)[None, :, None]
    first = here & opens[:, None, :]
    second = here & (alive & (rank % 2 == 1))[:, None, :]

    def of(mask, values, default):
        found = jnp.sum(jnp.where(mask, values[:, None, :] - default, 0), axis=2, dtype=jnp.int32)
        return found + default

    slots_of = jnp.broadcast_to(slot[None], rows.shape)
    return (
        of(first, rows, 0),
        of(first, slots_of, 0),
        of(second, slots_of, 0),
        of(first, cols, spare),
        of(second, cols, spare),
        jnp.sum(opens, axis=1, dtype=jnp.int32),
        live,
    )


def make_project(starts, count, out_total, resident):
    def kernel(rows, firsts, seconds, first_cols, second_cols, pairs, live, origin, *rest):
        parts, rest = rest[: len(starts)], rest[len(starts) :]
        sources, outs = rest[:CORES], rest[-3 - out_total : -3]
        blocks, total, sems = rest[-3:]
        width, depth = blocks.shape[2:]
        halves = parts[0].shape[2] // width
        size = count // len(starts)

        def meanwhile():
            total[...] = jnp.zeros_like(total)

        def body(side, places):
            terms = []
            for p in places:
                row = rows[side, p]
                at = pl.ds(pl.multiple_of((row % halves) * width, width), width)
                lhs = [part[row // halves, pl.ds(s, size), at] for part, s in zip(parts, starts)]
                lhs = lhs[0] if len(lhs) == 1 else jnp.concatenate(lhs, axis=0)
                held_in = sources[side] if side < resident else blocks.at[side]
                rhs = [held_in[firsts[side, p]], held_in[seconds[side, p]]]
                rhs = jnp.concatenate(rhs, axis=1)
                terms.append(jnp.dot(lhs, rhs, preferred_element_type=jnp.float32))
            for p, term in zip(places, terms):
                total[first_cols[side, p]] += term[:, :depth]
                total[second_cols[side, p]] += term[:, depth:]

        each_pair(sources, blocks, sems, live, pairs, meanwhile, body, resident)
        share = count // len(outs)
        for mask, out in enumerate(outs):
            start = pl.multiple_of((origin[0] ^ mask) * share, share)
            out[...] = total[: out.shape[0], pl.ds(start, share), :].astype(out.dtype)

    return kernel


def make_apply(part_total, earlier_total, out_total):
    def kernel(rows, firsts, seconds, first_cols, second_cols, pairs, live, origin, *rest):
        parts, rest = rest[:part_total], rest[part_total:]
        sources, rest = rest[:CORES], rest[CORES:]
        earlier, outs = rest[:earlier_total], rest[-4 - out_total : -4]
        blocks, chi, total, sems = rest[-4:]
        width = blocks.shape[2]
        halves = outs[0].shape[2] // width
        count = total.shape[1]
        share = count // part_total

        def meanwhile():
            total[...] = jnp.zeros_like(total)
            spare = parts[0].shape[0]
            chi[spare] = jnp.zeros_like(chi[spare])
            for mask, part in enumerate(parts):
                chi[:spare, mask * share : (mask + 1) * share, :] = part[...]
            for value, out in zip(earlier, outs):
                out[:, : value.shape[1], :] = value[...]

        def body(side, places):
            terms = []
            for p in places:
                lhs = jnp.concatenate([chi[first_cols[side, p]], chi[second_cols[side, p]]], axis=1)
                rhs = [blocks[side, firsts[side, p]], blocks[side, seconds[side, p]]]
                rhs = jnp.concatenate(rhs, axis=1)
                dims = (((1,), (1,)), ((), ()))
                terms.append(lax.dot_general(lhs, rhs, dims, preferred_element_type=jnp.float32))
            for p, term in zip(places, terms):
                total[rows[side, p]] += term

        each_pair(sources, blocks, sems, live, pairs, meanwhile, body)
        for place in range(part_total):
            start = pl.multiple_of((origin[0] ^ place) * share, share)
            out = outs[place % len(outs)]
            to = pl.ds(out.shape[1] - share if len(outs) > 1 else place * share, share)
            for row in range(total.shape[0]):
                at = pl.ds((row % halves) * width, width)
                out[row // halves, to, at] = total[row, pl.ds(start, share), :].astype(out.dtype)

    return kernel


def options(weights, count):
    slots, height, width = weights.shape
    return dict(
        compiler_params=pltpu.CompilerParams(vmem_limit_bytes=VMEM_BYTES),
        cost_estimate=pl.CostEstimate(
            flops=2 * CORES * slots * height * width * count,
            bytes_accessed=CORES * weights.size * 2 + 4 * 1024 * 1024,
            transcendentals=0,
        ),
    )


def held(weights):
    slots = weights[0].shape[0]
    return (
        pltpu.VMEM((CORES,) + weights[0].shape, weights[0].dtype),
        pltpu.SemaphoreType.DMA((CORES, 6 if slots % 6 == 0 else 1)),
    )


def keep_kernel(source, out, sem):
    copy = pltpu.make_async_copy(source, out, sem)
    copy.start()
    copy.wait()


def kept(value):
    return pl.pallas_call(
        keep_kernel,
        out_shape=jax.ShapeDtypeStruct(value.shape, value.dtype),
        in_specs=[APART],
        out_specs=WHOLE,
        scratch_shapes=[pltpu.SemaphoreType.DMA],
        compiler_params=pltpu.CompilerParams(vmem_limit_bytes=SMALL_BYTES),
    )(value)


def project(index, parts, starts, count, weights, after, col_total, parties, resident):
    width = weights[0].shape[2]
    blocks, sems = held(weights)
    kinds = [jnp.float32] + [jnp.bfloat16] * (parties - 1)
    return pl.pallas_call(
        make_project(starts, count, parties, resident),
        out_shape=[jax.ShapeDtypeStruct((col_total, count // parties, width), k) for k in kinds],
        in_specs=[SCALARS] * len(index)
        + [WHOLE] * (len(parts) + resident)
        + [APART] * (CORES - resident)
        + [ANYWHERE] * len(after),
        out_specs=[WHOLE] * parties,
        scratch_shapes=[blocks, pltpu.VMEM((col_total + 1, count, width), jnp.float32), sems],
        **options(weights[0], count),
    )(*index, *parts, *weights, *after)


def add_kernel(own, *rest):
    scaling, low, high = rest[-3:]
    value = own[...]
    for share in rest[:-3]:
        value = value + share[...].astype(jnp.float32)
    half = value.shape[0] // 2
    cols = scaling.shape[0] // CORES
    low[:half] = value[:half]
    high[:half] = value[half:]
    low[half, :cols] = scaling[:cols]
    high[half, :cols] = scaling[cols:]


def added(shares, scaling):
    total, rows, width = shares[0].shape
    shape = jax.ShapeDtypeStruct((total // 2 + 1, rows, width), jnp.float32)
    return pl.pallas_call(
        add_kernel,
        out_shape=[shape, shape],
        in_specs=[WHOLE] * (len(shares) + 1),
        out_specs=[WHOLE] * 2,
        compiler_params=pltpu.CompilerParams(vmem_limit_bytes=SMALL_BYTES),
    )(*shares, scaling)


def scale_kernel(low, high, below, above, out):
    half = low.shape[0] - 1
    cols = half // 2
    for at, own, other, couplings in (
        (0, low, below, (below, low)),
        (half, high, above, (high, above)),
    ):
        for side, source in enumerate(couplings):
            for c in range(cols):
                k = side * cols + c
                scale = source[half, c : c + 1, :]
                out[at + k] = (scale * (own[k] + other[k])).astype(jnp.bfloat16)


def scaled(low, high, below, above):
    blocks, rows, width = low.shape
    return pl.pallas_call(
        scale_kernel,
        out_shape=jax.ShapeDtypeStruct((2 * (blocks - 1), rows, width), jnp.bfloat16),
        in_specs=[WHOLE] * 4,
        out_specs=WHOLE,
        compiler_params=pltpu.CompilerParams(vmem_limit_bytes=SMALL_BYTES),
    )(low, high, below, above)


def apply(index, parts, weights, earlier, after, shapes):
    planes, _, points = shapes[0]
    col_total, rows, width = parts[0].shape
    count = rows * len(parts)
    height = weights[0].shape[1]
    blocks, sems = held(weights)
    return pl.pallas_call(
        make_apply(len(parts), len(earlier), len(shapes)),
        out_shape=[jax.ShapeDtypeStruct(shape, jnp.bfloat16) for shape in shapes],
        in_specs=[SCALARS] * len(index)
        + [WHOLE] * len(parts)
        + [APART] * CORES
        + [WHOLE] * len(earlier)
        + [ANYWHERE] * len(after),
        out_specs=[WHOLE] * len(shapes),
        scratch_shapes=[
            blocks,
            pltpu.VMEM((col_total + 1, count, width), jnp.bfloat16),
            pltpu.VMEM((planes * points // height, count, height), jnp.float32),
            sems,
        ],
        **options(weights[0], count),
    )(*index, *parts, *weights, *earlier, *after)


def per_device(orbitals, projector_blocks, block_rows, block_cols, block_counts, strengths):
    slabs = lax.axis_size("dom")
    parties = lax.axis_size("band")
    chips = slabs // CORES
    local, all_planes, points = orbitals.shape
    planes = all_planes // chips
    weights = projector_blocks[0, 0]
    slots, height, width = weights.shape
    col_blocks = strengths.shape[0] // width
    row_blocks = planes * points // height // CORES
    band = lax.axis_index("band").astype(jnp.int32)
    place = lax.axis_index("dom").astype(jnp.int32)
    core, chip = place % CORES, place // CORES
    sizes = CHUNKS if sum(CHUNKS) == local else (local,)
    direct = DIRECT and chips == parties and all(size % 16 == 0 for size in sizes)
    sizes = sizes if direct else (local,)
    firsts = [sum(sizes[:i]) for i in range(len(sizes))]

    def across(value, steps):
        return shifted(value, "dom", CORES * steps)

    groups = [[CORES * i + c for i in range(chips)] for c in range(CORES)]

    def taken(source, first, size, mask):
        piece = lax.dynamic_slice(source, (first, (chip ^ mask) * planes, 0), (size, planes, points))
        return piece.transpose(1, 0, 2)

    def brought():
        if not direct:
            piece = orbitals.reshape(local, chips, planes, points).transpose(1, 2, 0, 3)
            states = lax.all_to_all(piece, "dom", 0, 0, axis_index_groups=groups, tiled=True)
            return [([states.transpose(1, 0, 2, 3).reshape(planes, chips * local, points)], [0])]
        source, near, far = orbitals, {}, [{} for _ in sizes]
        for chunk, (first, size) in enumerate(zip(firsts, sizes)):
            for mask in ORDER:
                if mask <= NEAR and chunk:
                    continue
                span = (0, local) if mask <= NEAR else (first, size)
                piece = taken(source, *span, mask)
                (near if mask <= NEAR else far[chunk])[mask] = piece
        near = {mask: swapped(piece, "dom", CORES * mask) if mask else piece for mask, piece in near.items()}
        for chunk, pieces in enumerate(far):
            masks = [mask for mask in ORDER if mask in pieces]
            if chunk and HOLD:
                earlier = far[chunk - 1]
                tied = [pieces[mask] for mask in masks] + [earlier[mask] for mask in HOLD]
                tied = lax.optimization_barrier(tuple(tied))
                pieces.update(zip(masks, tied))
                earlier.update(zip(HOLD, tied[len(masks) :]))
            for mask in masks:
                pieces[mask] = swapped(pieces[mask], "dom", CORES * mask)
        chunks = []
        for first, pieces in zip(firsts, far):
            held_in = [near.get(mask, pieces.get(mask)) for mask in range(chips)]
            chunks.append((held_in, [first if mask <= NEAR else 0 for mask in range(chips)]))
        return chunks

    def returned(results):
        if not direct:
            result = results[0][0].reshape(planes, chips, local, points).transpose(1, 0, 2, 3)
            result = lax.all_to_all(result, "dom", 0, 0, axis_index_groups=groups, tiled=True)
            return result.reshape(all_planes, local, points).transpose(1, 0, 2)
        pieces = []
        for first, size, result in zip(firsts, sizes, results):
            for mask in range(NEAR + 1, chips):
                pieces.append((first, mask, swapped(result[mask], "dom", CORES * mask)))
        for mask in range(NEAR + 1):
            part = results[-1][mask]
            pieces.append((0, mask, swapped(part, "dom", CORES * mask) if mask else part))
        whole = jnp.zeros(orbitals.shape, orbitals.dtype)
        for first, mask, part in pieces:
            start = (first, (chip ^ mask) * planes, 0)
            whole = lax.dynamic_update_slice(whole, part.transpose(1, 0, 2), start)
        return whole

    numbers = jnp.concatenate(
        [
            block_rows.reshape(-1).astype(jnp.float32),
            block_cols.reshape(-1).astype(jnp.float32),
            block_counts.reshape(-1).astype(jnp.float32),
            strengths,
        ]
    )
    pair = jnp.stack([numbers, swapped(numbers, "dom", 1)])
    sides = jnp.stack([core, 1 - core])[:, None]
    index = paired(
        pair[:, :slots].astype(jnp.int32) + sides * row_blocks,
        pair[:, slots : 2 * slots].astype(jnp.int32) + sides * col_blocks,
        pair[:, 2 * slots].astype(jnp.int32),
        row_blocks,
        (CORES + 2) * col_blocks,
    )
    index = index + ((band ^ chip if direct else band).reshape(1),)
    scaling = pair[:, 2 * slots + 1 :]
    ends = [jnp.where(core == c, scaling[0], scaling[1]) for c in range(CORES)]
    scaling = jnp.concatenate(ends).reshape(CORES * col_blocks, width)
    both = (weights, swapped(weights, "dom", 1))

    col_total = (CORES + 2) * col_blocks
    chis, token = [], []
    for size, (parts, starts) in zip(sizes, brought()):
        count = size * chips
        resident = 0 if chis or not direct else RESIDENT
        used = [kept(value) if side < resident else value for side, value in enumerate(both)]
        own, *sends = project(index, parts, starts, count, used, token, col_total, parties, resident)
        shares = [swapped(send, "band", mask) for mask, send in enumerate(sends, 1)]
        low, high = added([own] + shares, scaling)
        below, above = lax.optimization_barrier((across(high, 1), across(low, -1)))
        chi = scaled(low, high, below, above)
        parts = [chi] + [swapped(chi, "band", mask) for mask in range(1, parties)]
        chis.append(parts)
        token = [(low, chi, parts[-1])[AFTER]]
        lasts = [[], [low], [chi]][LAST]
    results, earlier = [], []
    for first, size, parts in zip(firsts, sizes, chis):
        if direct:
            shapes = [(planes, size + (first if mask <= NEAR else 0), points) for mask in range(chips)]
        else:
            shapes = [(planes, chips * size, points)]
        results.append(apply(index, parts, both, earlier, lasts, shapes))
        earlier = results[-1][: NEAR + 1]
    return returned(results)


def solution(mesh):
    return jax.shard_map(
        per_device,
        mesh=mesh,
        in_specs=(
            P("dom", None, "band"),
            P("band", "dom", None, None, None),
            P("band", "dom", None),
            P("band", "dom", None),
            P("band", "dom"),
            P("dom"),
        ),
        out_specs=P("dom", None, "band"),
        check_vma=False,
    )
```

```python
import jax
import jax.numpy as jnp
from jax import lax
from jax.experimental import pallas as pl
from jax.experimental.pallas import tpu as pltpu
from jax.sharding import PartitionSpec as P

CHUNKS = (16, 16)
DIRECT = True
NEAR = 1
AFTER = 0
LAST = 1
ORDER = (3, 2, 1, 0)
HOLD = (2,)
PINNED = True
VMEM_BYTES = 24 * 1024 * 1024
SMALL_BYTES = 8 * 1024 * 1024
WIDTH = 8
WHOLE = pl.BlockSpec(memory_space=pltpu.VMEM)
SCALARS = pl.BlockSpec(memory_space=pltpu.SMEM)
ANYWHERE = pl.BlockSpec(memory_space=pl.ANY)
APART = pl.BlockSpec(memory_space=pltpu.HBM) if PINNED else ANYWHERE
CORES = 2


def shifted(value, axis, steps):
    count = lax.axis_size(axis)
    return lax.ppermute(value, axis, [(i, (i + steps) % count) for i in range(count)])


def swapped(value, axis, mask):
    count = lax.axis_size(axis)
    return lax.ppermute(value, axis, [(i, i ^ mask) for i in range(count)])


def each_pair(sources, blocks, sems, live, pairs, meanwhile, body):
    per = sems.shape[1]
    step = blocks.shape[1] // per

    def each_copy(side, act):
        for i in range(per):
            span = pl.ds(i * step, step)

            @pl.when(live[side] > i * step)
            def _():
                copy = pltpu.make_async_copy(sources[side].at[span], blocks.at[side, span], sems.at[side, i])
                act(copy)

    lighter = jnp.where(live[1] < live[0], 1, 0)
    order = [lighter, 1 - lighter]
    for turn in order:
        for side in range(len(sources)):

            @pl.when(turn == side)
            def _():
                each_copy(side, lambda copy: copy.start())

    meanwhile()
    for turn in order:
        for i in range(per):
            span = pl.ds(i * step, step)

            @pl.when(live[turn] > i * step)
            def _():
                pltpu.make_async_copy(sources[0].at[span], blocks.at[turn, span], sems.at[turn, i]).wait()

        @pl.loop(0, (pairs[turn] + WIDTH - 1) // WIDTH)
        def _(g):
            body(turn, [g * WIDTH + t for t in range(WIDTH)])


def paired(rows, cols, live, row_blocks, spare):
    slots = rows.shape[1]
    slot = jnp.arange(slots, dtype=jnp.int32)
    place_total = -(-(slots + row_blocks) // 2 // WIDTH) * WIDTH
    alive = slot[None] < live[:, None]
    same = (rows[:, :, None] == rows[:, None, :]) & alive[:, None, :]
    rank = jnp.sum(same & (slot[None, None, :] < slot[None, :, None]), axis=2, dtype=jnp.int32)
    opens = alive & (rank % 2 == 0)
    lower = opens[:, None, :] & (rows[:, None, :] < rows[:, :, None])
    pair = jnp.sum(lower, axis=2, dtype=jnp.int32) + rank // 2
    here = pair[:, None, :] == jnp.arange(place_total, dtype=jnp.int32)[None, :, None]
    first = here & opens[:, None, :]
    second = here & (alive & (rank % 2 == 1))[:, None, :]

    def of(mask, values, default):
        found = jnp.sum(jnp.where(mask, values[:, None, :] - default, 0), axis=2, dtype=jnp.int32)
        return found + default

    slots_of = jnp.broadcast_to(slot[None], rows.shape)
    return (
        of(first, rows, 0),
        of(first, slots_of, 0),
        of(second, slots_of, 0),
        of(first, cols, spare),
        of(second, cols, spare),
        jnp.sum(opens, axis=1, dtype=jnp.int32),
        live,
    )


def make_project(starts, count, out_total):
    def kernel(rows, firsts, seconds, first_cols, second_cols, pairs, live, origin, *rest):
        parts, rest = rest[: len(starts)], rest[len(starts) :]
        sources, outs = rest[:CORES], rest[-3 - out_total : -3]
        blocks, total, sems = rest[-3:]
        width, depth = blocks.shape[2:]
        halves = parts[0].shape[2] // width
        size = count // len(starts)

        def meanwhile():
            total[...] = jnp.zeros_like(total)

        def body(side, places):
            terms = []
            for p in places:
                row = rows[side, p]
                at = pl.ds(pl.multiple_of((row % halves) * width, width), width)
                lhs = [part[row // halves, pl.ds(s, size), at] for part, s in zip(parts, starts)]
                lhs = lhs[0] if len(lhs) == 1 else jnp.concatenate(lhs, axis=0)
                rhs = [blocks[side, firsts[side, p]], blocks[side, seconds[side, p]]]
                rhs = jnp.concatenate(rhs, axis=1)
                terms.append(jnp.dot(lhs, rhs, preferred_element_type=jnp.float32))
            for p, term in zip(places, terms):
                total[first_cols[side, p]] += term[:, :depth]
                total[second_cols[side, p]] += term[:, depth:]

        each_pair(sources, blocks, sems, live, pairs, meanwhile, body)
        share = count // len(outs)
        for mask, out in enumerate(outs):
            start = pl.multiple_of((origin[0] ^ mask) * share, share)
            out[...] = total[: out.shape[0], pl.ds(start, share), :].astype(out.dtype)

    return kernel


def make_apply(part_total, earlier_total, out_total):
    def kernel(rows, firsts, seconds, first_cols, second_cols, pairs, live, origin, *rest):
        parts, rest = rest[:part_total], rest[part_total:]
        sources, rest = rest[:CORES], rest[CORES:]
        earlier, outs = rest[:earlier_total], rest[-4 - out_total : -4]
        blocks, chi, total, sems = rest[-4:]
        width = blocks.shape[2]
        halves = outs[0].shape[2] // width
        count = total.shape[1]
        share = count // part_total

        def meanwhile():
            total[...] = jnp.zeros_like(total)
            spare = parts[0].shape[0]
            chi[spare] = jnp.zeros_like(chi[spare])
            for mask, part in enumerate(parts):
                chi[:spare, mask * share : (mask + 1) * share, :] = part[...]
            for value, out in zip(earlier, outs):
                out[:, : value.shape[1], :] = value[...]

        def body(side, places):
            terms = []
            for p in places:
                lhs = jnp.concatenate([chi[first_cols[side, p]], chi[second_cols[side, p]]], axis=1)
                rhs = [blocks[side, firsts[side, p]], blocks[side, seconds[side, p]]]
                rhs = jnp.concatenate(rhs, axis=1)
                dims = (((1,), (1,)), ((), ()))
                terms.append(lax.dot_general(lhs, rhs, dims, preferred_element_type=jnp.float32))
            for p, term in zip(places, terms):
                total[rows[side, p]] += term

        each_pair(sources, blocks, sems, live, pairs, meanwhile, body)
        for place in range(part_total):
            start = pl.multiple_of((origin[0] ^ place) * share, share)
            out = outs[place % len(outs)]
            to = pl.ds(out.shape[1] - share if len(outs) > 1 else place * share, share)
            for row in range(total.shape[0]):
                at = pl.ds((row % halves) * width, width)
                out[row // halves, to, at] = total[row, pl.ds(start, share), :].astype(out.dtype)

    return kernel


def options(weights, count):
    slots, height, width = weights.shape
    return dict(
        compiler_params=pltpu.CompilerParams(vmem_limit_bytes=VMEM_BYTES),
        cost_estimate=pl.CostEstimate(
            flops=2 * CORES * slots * height * width * count,
            bytes_accessed=CORES * weights.size * 2 + 4 * 1024 * 1024,
            transcendentals=0,
        ),
    )


def held(weights):
    slots = weights[0].shape[0]
    return (
        pltpu.VMEM((CORES,) + weights[0].shape, weights[0].dtype),
        pltpu.SemaphoreType.DMA((CORES, 6 if slots % 6 == 0 else 1)),
    )


def project(index, parts, starts, count, weights, after, col_total, parties):
    width = weights[0].shape[2]
    blocks, sems = held(weights)
    kinds = [jnp.float32] + [jnp.bfloat16] * (parties - 1)
    return pl.pallas_call(
        make_project(starts, count, parties),
        out_shape=[jax.ShapeDtypeStruct((col_total, count // parties, width), k) for k in kinds],
        in_specs=[SCALARS] * len(index) + [WHOLE] * len(parts) + [APART] * CORES + [ANYWHERE] * len(after),
        out_specs=[WHOLE] * parties,
        scratch_shapes=[blocks, pltpu.VMEM((col_total + 1, count, width), jnp.float32), sems],
        **options(weights[0], count),
    )(*index, *parts, *weights, *after)


def add_kernel(own, *rest):
    scaling, low, high = rest[-3:]
    value = own[...]
    for share in rest[:-3]:
        value = value + share[...].astype(jnp.float32)
    half = value.shape[0] // 2
    cols = scaling.shape[0] // CORES
    low[:half] = value[:half]
    high[:half] = value[half:]
    low[half, :cols] = scaling[:cols]
    high[half, :cols] = scaling[cols:]


def added(shares, scaling):
    total, rows, width = shares[0].shape
    shape = jax.ShapeDtypeStruct((total // 2 + 1, rows, width), jnp.float32)
    return pl.pallas_call(
        add_kernel,
        out_shape=[shape, shape],
        in_specs=[WHOLE] * (len(shares) + 1),
        out_specs=[WHOLE] * 2,
        compiler_params=pltpu.CompilerParams(vmem_limit_bytes=SMALL_BYTES),
    )(*shares, scaling)


def scale_kernel(low, high, below, above, out):
    half = low.shape[0] - 1
    cols = half // 2
    for at, own, other, couplings in (
        (0, low, below, (below, low)),
        (half, high, above, (high, above)),
    ):
        for side, source in enumerate(couplings):
            for c in range(cols):
                k = side * cols + c
                scale = source[half, c : c + 1, :]
                out[at + k] = (scale * (own[k] + other[k])).astype(jnp.bfloat16)


def scaled(low, high, below, above):
    blocks, rows, width = low.shape
    return pl.pallas_call(
        scale_kernel,
        out_shape=jax.ShapeDtypeStruct((2 * (blocks - 1), rows, width), jnp.bfloat16),
        in_specs=[WHOLE] * 4,
        out_specs=WHOLE,
        compiler_params=pltpu.CompilerParams(vmem_limit_bytes=SMALL_BYTES),
    )(low, high, below, above)


def apply(index, parts, weights, earlier, after, shapes):
    planes, _, points = shapes[0]
    col_total, rows, width = parts[0].shape
    count = rows * len(parts)
    height = weights[0].shape[1]
    blocks, sems = held(weights)
    return pl.pallas_call(
        make_apply(len(parts), len(earlier), len(shapes)),
        out_shape=[jax.ShapeDtypeStruct(shape, jnp.bfloat16) for shape in shapes],
        in_specs=[SCALARS] * len(index)
        + [WHOLE] * len(parts)
        + [APART] * CORES
        + [WHOLE] * len(earlier)
        + [ANYWHERE] * len(after),
        out_specs=[WHOLE] * len(shapes),
        scratch_shapes=[
            blocks,
            pltpu.VMEM((col_total + 1, count, width), jnp.bfloat16),
            pltpu.VMEM((planes * points // height, count, height), jnp.float32),
            sems,
        ],
        **options(weights[0], count),
    )(*index, *parts, *weights, *earlier, *after)


def per_device(orbitals, projector_blocks, block_rows, block_cols, block_counts, strengths):
    slabs = lax.axis_size("dom")
    parties = lax.axis_size("band")
    chips = slabs // CORES
    local, all_planes, points = orbitals.shape
    planes = all_planes // chips
    weights = projector_blocks[0, 0]
    slots, height, width = weights.shape
    col_blocks = strengths.shape[0] // width
    row_blocks = planes * points // height // CORES
    band = lax.axis_index("band").astype(jnp.int32)
    place = lax.axis_index("dom").astype(jnp.int32)
    core, chip = place % CORES, place // CORES
    sizes = CHUNKS if sum(CHUNKS) == local else (local,)
    direct = DIRECT and chips == parties and all(size % 16 == 0 for size in sizes)
    sizes = sizes if direct else (local,)
    firsts = [sum(sizes[:i]) for i in range(len(sizes))]

    def across(value, steps):
        return shifted(value, "dom", CORES * steps)

    groups = [[CORES * i + c for i in range(chips)] for c in range(CORES)]

    def taken(source, first, size, mask):
        piece = lax.dynamic_slice(source, (first, (chip ^ mask) * planes, 0), (size, planes, points))
        return piece.transpose(1, 0, 2)

    def brought():
        if not direct:
            piece = orbitals.reshape(local, chips, planes, points).transpose(1, 2, 0, 3)
            states = lax.all_to_all(piece, "dom", 0, 0, axis_index_groups=groups, tiled=True)
            return [([states.transpose(1, 0, 2, 3).reshape(planes, chips * local, points)], [0])]
        source, near, far = orbitals, {}, [{} for _ in sizes]
        for chunk, (first, size) in enumerate(zip(firsts, sizes)):
            for mask in ORDER:
                if mask <= NEAR and chunk:
                    continue
                span = (0, local) if mask <= NEAR else (first, size)
                piece = taken(source, *span, mask)
                (near if mask <= NEAR else far[chunk])[mask] = piece
        near = {mask: swapped(piece, "dom", CORES * mask) if mask else piece for mask, piece in near.items()}
        for chunk, pieces in enumerate(far):
            masks = [mask for mask in ORDER if mask in pieces]
            if chunk and HOLD:
                earlier = far[chunk - 1]
                tied = [pieces[mask] for mask in masks] + [earlier[mask] for mask in HOLD]
                tied = lax.optimization_barrier(tuple(tied))
                pieces.update(zip(masks, tied))
                earlier.update(zip(HOLD, tied[len(masks) :]))
            for mask in masks:
                pieces[mask] = swapped(pieces[mask], "dom", CORES * mask)
        chunks = []
        for first, pieces in zip(firsts, far):
            held_in = [near.get(mask, pieces.get(mask)) for mask in range(chips)]
            chunks.append((held_in, [first if mask <= NEAR else 0 for mask in range(chips)]))
        return chunks

    def returned(results):
        if not direct:
            result = results[0][0].reshape(planes, chips, local, points).transpose(1, 0, 2, 3)
            result = lax.all_to_all(result, "dom", 0, 0, axis_index_groups=groups, tiled=True)
            return result.reshape(all_planes, local, points).transpose(1, 0, 2)
        pieces = []
        for first, size, result in zip(firsts, sizes, results):
            for mask in range(NEAR + 1, chips):
                pieces.append((first, mask, swapped(result[mask], "dom", CORES * mask)))
        for mask in range(NEAR + 1):
            part = results[-1][mask]
            pieces.append((0, mask, swapped(part, "dom", CORES * mask) if mask else part))
        whole = jnp.zeros(orbitals.shape, orbitals.dtype)
        for first, mask, part in pieces:
            start = (first, (chip ^ mask) * planes, 0)
            whole = lax.dynamic_update_slice(whole, part.transpose(1, 0, 2), start)
        return whole

    numbers = jnp.concatenate(
        [
            block_rows.reshape(-1).astype(jnp.float32),
            block_cols.reshape(-1).astype(jnp.float32),
            block_counts.reshape(-1).astype(jnp.float32),
            strengths,
        ]
    )
    pair = jnp.stack([numbers, swapped(numbers, "dom", 1)])
    sides = jnp.stack([core, 1 - core])[:, None]
    index = paired(
        pair[:, :slots].astype(jnp.int32) + sides * row_blocks,
        pair[:, slots : 2 * slots].astype(jnp.int32) + sides * col_blocks,
        pair[:, 2 * slots].astype(jnp.int32),
        row_blocks,
        (CORES + 2) * col_blocks,
    )
    index = index + ((band ^ chip if direct else band).reshape(1),)
    scaling = pair[:, 2 * slots + 1 :]
    ends = [jnp.where(core == c, scaling[0], scaling[1]) for c in range(CORES)]
    scaling = jnp.concatenate(ends).reshape(CORES * col_blocks, width)
    both = (weights, swapped(weights, "dom", 1))

    col_total = (CORES + 2) * col_blocks
    chis, token = [], []
    for size, (parts, starts) in zip(sizes, brought()):
        count = size * chips
        own, *sends = project(index, parts, starts, count, both, token, col_total, parties)
        shares = [swapped(send, "band", mask) for mask, send in enumerate(sends, 1)]
        low, high = added([own] + shares, scaling)
        below, above = lax.optimization_barrier((across(high, 1), across(low, -1)))
        chi = scaled(low, high, below, above)
        parts = [chi] + [swapped(chi, "band", mask) for mask in range(1, parties)]
        chis.append(parts)
        token = [(low, chi, parts[-1])[AFTER]]
        lasts = [[], [low], [chi]][LAST]
    results, earlier = [], []
    for first, size, parts in zip(firsts, sizes, chis):
        if direct:
            shapes = [(planes, size + (first if mask <= NEAR else 0), points) for mask in range(chips)]
        else:
            shapes = [(planes, chips * size, points)]
        results.append(apply(index, parts, both, earlier, lasts, shapes))
        earlier = results[-1][: NEAR + 1]
    return returned(results)


def solution(mesh):
    return jax.shard_map(
        per_device,
        mesh=mesh,
        in_specs=(
            P("dom", None, "band"),
            P("band", "dom", None, None, None),
            P("band", "dom", None),
            P("band", "dom", None),
            P("band", "dom"),
            P("dom"),
        ),
        out_specs=P("dom", None, "band"),
        check_vma=False,
    )
```
